32 devices in a mesh: groups: 2 (over y), ex: 4 (over z), layer: 4 (over x, core).
Axes of the slice: x: 2, y: 2, z: 4, core: 2. Of those that a mesh axis runs over, the one named last changes fastest.
Arguments:
- queries: bfloat16 [256, 16384], P('ex', 'layer'), may hold values from -6 to 6
- train_grads: bfloat16 [3072, 16384], P(('groups', 'ex'), 'layer'), parts along dimension 0, may hold values from -1800 to 1800
- layer_start: int32 [32], replicated, may hold values from 0 to 16128, as said below
Outputs:
- scores: float32 [3072, 256], P(('groups', 'ex', 'layer')), parts along dimension 0
The draws below stay inside these ranges and needn't reach their ends.
There are 2 independent parts, one for each index of `groups`. The reference program is written for one: setup_inputs(seed, part) draws one part's arguments, and reference() takes and returns one part's arrays. A program takes and returns all parts, laid end to end along the dimension named above; an argument that names none is the same for every part. Nothing has to cross between parts.
Inputs may be any that keep to these rules, and one draw needn't show every extreme that they name: layer_start[0] is 0 and it rises; each layer has 256 to 3 * (256) columns, both bounds reached, and the layers end at 16384.
All inputs are finite; a program needn't handle non-finite values.
Results may differ from the reference program's by a relative error of at most 0.0029.
Values may be sent and summed in bfloat16 or wider, within the bound.
A program may use at most 64 MiB of HBM per device.

```python
import math
import jax
import jax.numpy as jnp
from jax import lax

WIDTH = 16384
LAYERS = 32
EX_DEV = 384
QUERIES = 256
EXAMPLES = 1536
N_EX = 4


def draw_train_grads(key, part):
    key = jax.random.fold_in(key, 11)
    key_base, key_rows, key_cols = jax.random.split(key, 3)
    position = jnp.arange(WIDTH, dtype=jnp.float32) / WIDTH
    col_scale = jnp.exp(jax.random.uniform(key_cols, (1, WIDTH)) * math.log(10.0)) * (1.0 + 2.0 * position[None, :])
    row_scale = jnp.exp(jax.random.uniform(key_rows, (EXAMPLES, 1)) * math.log(10.0))
    base = jnp.clip(jax.random.normal(key_base, (EXAMPLES, WIDTH)), -6.0, 6.0)
    return (base * row_scale * col_scale).astype(jnp.bfloat16)


def draw_layer_start(key, part):
    key = jax.random.fold_in(key, 23)
    key_swing, key_shuffle = jax.random.split(key)
    mean_cols = WIDTH // LAYERS
    swing_cols = jax.random.randint(key_swing, (LAYERS // 2,), 0, mean_cols // 2 + 1)
    swing_cols = swing_cols.at[0].set(mean_cols // 2)
    layer_cols = jnp.concatenate([mean_cols + swing_cols, mean_cols - swing_cols])
    shuffle = jax.random.permutation(key_shuffle, LAYERS)
    layer_cols = layer_cols[shuffle]
    return (jnp.cumsum(layer_cols) - layer_cols).astype(jnp.int32)


def steps_of(key, dims, cuts, least, high):
    loudness = 1.0
    for axis_at, parts in cuts:
        draws = jax.random.uniform(jax.random.fold_in(jax.random.fold_in(key, 6), axis_at), (parts,), jnp.float32, least / len(cuts), high / len(cuts))
        loudness = loudness * jnp.repeat(jnp.exp(draws), dims[axis_at] // parts).reshape((-1,) + (1,) * (len(dims) - 1 - axis_at))
    return loudness


def scatter_about(stream_key, shape, spread, most, pieces=(), held_as=jnp.bfloat16):
    values = jax.random.normal(stream_key, shape, jnp.float32) * spread
    if len(pieces) > 0:
        values = steps_of(stream_key, shape, pieces, -0.22, 0.18) * values
    return jnp.clip(values, min=-most, max=most).astype(held_as)


def setup_inputs(seed: int = 0, part: int = 0) -> dict:
    key_list = jax.random.split(jax.random.key(seed), 4)
    part_keys = jax.random.split(jax.random.fold_in(key_list[3], part), 4)
    queries = scatter_about(key_list[0], (QUERIES, WIDTH), 1.0, 6.0, ((0, 4), (1, 4)))
    train_grads = draw_train_grads(jax.random.fold_in(jax.random.fold_in(key_list[3], part), 71), part)
    layer_start = draw_layer_start(jax.random.fold_in(key_list[3], 71), part)
    return {"queries": queries, "train_grads": train_grads, "layer_start": layer_start}


EPSILON = 1e-05

def layer_table(layer_start):
    layer_end = jnp.concatenate([layer_start[1:], jnp.array([WIDTH], jnp.int32)])
    columns = jnp.arange(WIDTH, dtype=jnp.int32)
    inside = (columns[:, None] >= layer_start[None, :]) & (columns[:, None] < layer_end[None, :])
    return (inside.astype(jnp.float32), (layer_end - layer_start).astype(jnp.float32))

def reference(queries, train_grads, layer_start):
    member, counts = layer_table(layer_start)
    blocks = train_grads.reshape(N_EX, EX_DEV, WIDTH)

    def score_block(grad_block):
        widened = grad_block.astype(jnp.float32)
        square_sums = jnp.dot(widened * widened, member, precision=lax.Precision.HIGHEST)
        overall = lax.optimization_barrier(jnp.sum(square_sums, axis=1, keepdims=True)) / WIDTH
        inv_norm = lax.rsqrt(square_sums / counts + overall + EPSILON) * WIDTH ** (-0.5)
        col_scale = jnp.dot(inv_norm, member.T, precision=lax.Precision.HIGHEST)
        scaled = (widened * col_scale).astype(jnp.bfloat16)
        return jnp.dot(scaled, queries.T, preferred_element_type=jnp.float32)
    return lax.map(score_block, blocks).reshape(EXAMPLES, QUERIES)
```

```python
import functools

import jax
import jax.numpy as jnp
from jax import lax
from jax.experimental import pallas as pl
from jax.experimental.pallas import tpu as pltpu
from jax.sharding import PartitionSpec as P

WIDTH = 16384
EPSILON = 1e-05
MESH = pl.DeviceIdType.MESH
LANES = 128


def nt_dot(a, b):
    return lax.dot_general(a, b, (((1,), (1,)), ((), ())), preferred_element_type=jnp.float32)


def kernel(
    n, groups, parts, chunks, start_ref, q_ref, x_hbm, out_ref,
    x_v, scaled_v, q_all, sums, sums_in, inv_v, acc, acc_in,
    x_sem, q_sem, z_send, z_recv, y_send, y_recv, sum_send, sum_recv, acc_send, acc_recv,
):
    y, z, me = lax.axis_index("groups"), lax.axis_index("ex"), lax.axis_index("layer")
    rows, width = q_ref.shape
    share = rows // groups
    chunk = width // chunks
    examples = x_hbm.shape[0]
    kept = examples // parts
    layers = start_ref.shape[0]
    last = n - 2
    pairs = n // 2

    def cols(c):
        return pl.ds(c * chunk, chunk)

    def x_copy(c):
        return pltpu.make_async_copy(x_hbm.at[:, cols(c)], x_v.at[:, cols(c)], x_sem.at[c])

    def block_rows(b):
        return pl.ds(pl.multiple_of(b * rows, rows), rows)

    def share_rows(b, g):
        return pl.ds(pl.multiple_of(b * rows + g * share, share), share)

    def z_target(flow):
        return z + 1 if flow == 0 else z - 1

    def has_target(flow):
        return z + 1 < n if flow == 0 else z > 0

    def arriving(flow, s):
        return z - 1 - s if flow == 0 else z + 1 + s

    def arrives(flow, s):
        return z - 1 - s >= 0 if flow == 0 else z + 1 + s < n

    def z_copy(flow, s, c, b, own=False):
        there = q_all.at[share_rows(b, y), cols(c)]
        here = q_ref.at[pl.ds(pl.multiple_of(y * share, share), share), cols(c)] if own else there
        return pltpu.make_async_remote_copy(
            src_ref=here, dst_ref=there, send_sem=z_send.at[flow, s, c], recv_sem=z_recv.at[flow, s, c],
            device_id={"ex": z_target(flow)}, device_id_type=MESH)

    def y_copy(flow, s, g, c, b, owner):
        block = q_all.at[share_rows(b, owner), cols(c)]
        return pltpu.make_async_remote_copy(
            src_ref=block, dst_ref=block, send_sem=y_send.at[flow, s, g - 1, c], recv_sem=y_recv.at[flow, s, g - 1, c],
            device_id={"groups": lax.rem(y + g, groups)}, device_id_type=MESH)

    def sum_copy(r):
        return pltpu.make_async_remote_copy(
            src_ref=sums, dst_ref=sums_in.at[r - 1], send_sem=sum_send.at[r - 1], recv_sem=sum_recv.at[r - 1],
            device_id={"layer": lax.rem(me + r, parts)}, device_id_type=MESH)

    def acc_copy(k, r):
        to = lax.rem(me + r, parts)
        return pltpu.make_async_remote_copy(
            src_ref=acc.at[k, pl.ds(pl.multiple_of(to * kept, 8), kept)], dst_ref=acc_in.at[k, r - 1],
            send_sem=acc_send.at[k, r - 1], recv_sem=acc_recv.at[k, r - 1],
            device_id={"layer": to}, device_id_type=MESH)

    def handle(s, c):
        for flow in (1, 0):
            @pl.when(arrives(flow, s))
            def _():
                b = arriving(flow, s)
                z_copy(flow, s, c, b).wait_recv()
                for g in range(1, groups):
                    y_copy(flow, s, g, c, b, y).start()
                if s < last:
                    @pl.when(has_target(flow))
                    def _():
                        z_copy(flow, s + 1, c, b).start()

    def wait_y(s, c):
        for flow in (1, 0):
            @pl.when(arrives(flow, s))
            def _():
                b = arriving(flow, s)
                for g in range(1, groups):
                    y_copy(flow, s, g, c, b, lax.rem(y + groups - g, groups)).wait_recv()

    for c in range(chunks):
        x_copy(c).start()
    q_copy = pltpu.make_async_copy(q_ref, q_all.at[block_rows(z)], q_sem)
    q_copy.start()

    barrier = pltpu.get_barrier_semaphore()
    for flow in (0, 1):
        @pl.when(has_target(flow))
        def _():
            pl.semaphore_signal(barrier, inc=1, device_id={"ex": z_target(flow)}, device_id_type=MESH)
    for g in range(1, groups):
        pl.semaphore_signal(barrier, inc=1, device_id={"groups": lax.rem(y + g, groups)}, device_id_type=MESH)
    for r in range(1, parts):
        pl.semaphore_signal(barrier, inc=1, device_id={"layer": lax.rem(me + r, parts)}, device_id_type=MESH)
    peers = groups + parts - jnp.where(z == 0, 1, 0) - jnp.where(z == n - 1, 1, 0)
    pl.semaphore_wait(barrier, peers)

    for c in range(chunks):
        for flow in (1, 0):
            @pl.when(has_target(flow))
            def _():
                z_copy(flow, 0, c, z, own=True).start()

    starts = [start_ref[l] for l in range(layers)]
    ends = starts[1:] + [WIDTH]
    offset = me * width

    def table(index):
        low = jnp.full(index.shape, WIDTH, jnp.int32)
        high = jnp.full(index.shape, 0, jnp.int32)
        for l in range(layers):
            low = jnp.where(index == l, starts[l], low)
            high = jnp.where(index == l, ends[l], high)
        return low - offset, high - offset

    lane_low, lane_high = table(lax.broadcasted_iota(jnp.int32, (1, LANES), 1))
    sub = lax.broadcasted_iota(jnp.int32, (LANES, 1), 0)
    pieces = 3
    sub_low, sub_high = table(jnp.where(sub < pieces * layers, lax.rem(sub, layers), layers))

    total = jnp.zeros((examples, LANES), jnp.float32)
    for c in range(chunks):
        x_copy(c).wait()
        column = c * chunk + lax.broadcasted_iota(jnp.int32, (chunk, LANES), 0)
        member = ((column >= lane_low) & (column < lane_high)).astype(jnp.float32).astype(jnp.bfloat16)
        wide = x_v[:, cols(c)].astype(jnp.float32)
        square = wide * wide
        big = square.astype(jnp.bfloat16)
        small = (square - big.astype(jnp.float32)).astype(jnp.bfloat16)
        total += jnp.dot(big, member, preferred_element_type=jnp.float32)
        total += jnp.dot(small, member, preferred_element_type=jnp.float32)
        handle(0, c)
    sums[...] = total.T[:layers]
    for r in range(1, parts):
        sum_copy(r).start()

    q_copy.wait()
    own_pair = z // 2

    def pair_dot(k, p, c):
        pair = pl.ds(pl.multiple_of(p * 2 * rows, 2 * rows), 2 * rows)
        value = nt_dot(scaled_v[:, cols(c)], q_all[pair, cols(c)])
        if c == 0:
            acc[k] = value
        else:
            acc[k] += value

    def send_pair(k):
        for r in range(1, parts):
            acc_copy(k, r).start()

    for c in range(chunks):
        if last >= 1:
            handle(1, c)
        if c == 0:
            for r in range(1, parts):
                sum_copy(r).wait_recv()
            tot = sums[...]
            for r in range(1, parts):
                tot += sums_in[r - 1]
            low, high = sub_low[:layers], sub_high[:layers]
            counts = (high - low).astype(jnp.float32)
            overall = jnp.sum(tot, axis=0, keepdims=True) / WIDTH
            inv = lax.rsqrt(tot / counts + overall + EPSILON) * WIDTH ** (-0.5)
            split = []
            rest = inv
            for _ in range(pieces):
                piece = rest.astype(jnp.bfloat16).astype(jnp.float32)
                split.append(piece)
                rest = rest - piece
            split.append(jnp.zeros((LANES - pieces * layers, examples), jnp.float32))
            inv_v[...] = jnp.concatenate(split, axis=0).T.astype(jnp.bfloat16)
        column = c * chunk + lax.broadcasted_iota(jnp.int32, (LANES, chunk), 1)
        member = ((column >= sub_low) & (column < sub_high)).astype(jnp.float32).astype(jnp.bfloat16)
        scale = jnp.dot(inv_v[...], member, preferred_element_type=jnp.float32)
        scaled_v[:, cols(c)] = (x_v[:, cols(c)].astype(jnp.float32) * scale).astype(jnp.bfloat16)
        wait_y(0, c)
        pair_dot(0, own_pair, c)
    send_pair(0)

    ahead = z < n // 2
    last_pair = jnp.where(ahead, pairs - 1, 0)
    pair_of = [own_pair]
    for s in range(2, last):
        for c in range(chunks):
            handle(s, c)
    handle(last, 0)
    for s in range(1, last):
        for c in range(chunks):
            wait_y(s, c)
    for k in range(1, pairs - 1):
        p = jnp.where(ahead, k - 1, k)
        p = p + jnp.where(p >= own_pair, 1, 0)
        pair_of.append(p)
        for c in range(chunks):
            pair_dot(k, p, c)
        send_pair(k)
    pair_of.append(last_pair)
    for c in range(chunks):
        if c + 1 < chunks:
            handle(last, c + 1)
        wait_y(last, c)
        pair_dot(pairs - 1, last_pair, c)
    send_pair(pairs - 1)

    mine = pl.ds(pl.multiple_of(me * kept, 8), kept)
    for k in range(pairs):
        value = acc[k, mine]
        for r in range(1, parts):
            acc_copy(k, r).wait_recv()
            value += acc_in[k, r - 1]
        out_ref[:, pl.ds(pl.multiple_of(pair_of[k] * 2 * rows, 2 * rows), 2 * rows)] = value

    for r in range(1, parts):
        sum_copy(r).wait_send()
        for k in range(pairs):
            acc_copy(k, r).wait_send()
    for flow in (1, 0):
        for s in range(last + 1):
            for c in range(chunks):
                if s == 0:
                    @pl.when(has_target(flow))
                    def _():
                        z_copy(flow, 0, c, z, own=True).wait_send()

                @pl.when(arrives(flow, s))
                def _():
                    b = arriving(flow, s)
                    for g in range(1, groups):
                        y_copy(flow, s, g, c, b, y).wait_send()
                    if s < last:
                        @pl.when(has_target(flow))
                        def _():
                            z_copy(flow, s + 1, c, b).wait_send()


def solution(mesh):
    n, groups, parts = mesh.shape["ex"], mesh.shape["groups"], mesh.shape["layer"]
    chunks = max(1, 16 // n)

    def body(queries, train_grads, layer_start):
        rows, width = queries.shape
        examples = train_grads.shape[0]
        layers = layer_start.shape[0]
        kept = examples // parts
        pairs = n // 2
        dma = pltpu.SemaphoreType.DMA
        return pl.pallas_call(
            functools.partial(kernel, n, groups, parts, chunks),
            out_shape=jax.ShapeDtypeStruct((kept, n * rows), jnp.float32),
            in_specs=[
                pl.BlockSpec(memory_space=pltpu.SMEM),
                pl.BlockSpec(memory_space=pl.ANY),
                pl.BlockSpec(memory_space=pl.ANY),
            ],
            out_specs=pl.BlockSpec(memory_space=pltpu.VMEM),
            scratch_shapes=[
                pltpu.VMEM((examples, width), jnp.bfloat16),
                pltpu.VMEM((examples, width), jnp.bfloat16),
                pltpu.VMEM((n * rows, width), jnp.bfloat16),
                pltpu.VMEM((layers, examples), jnp.float32),
                pltpu.VMEM((parts - 1, layers, examples), jnp.float32),
                pltpu.VMEM((examples, LANES), jnp.bfloat16),
                pltpu.VMEM((pairs, examples, 2 * rows), jnp.float32),
                pltpu.VMEM((pairs, parts - 1, kept, 2 * rows), jnp.float32),
                dma((chunks,)),
                dma,
                dma((2, n - 1, chunks)),
                dma((2, n - 1, chunks)),
                dma((2, n - 1, groups - 1, chunks)),
                dma((2, n - 1, groups - 1, chunks)),
                dma((parts - 1,)),
                dma((parts - 1,)),
                dma((pairs, parts - 1)),
                dma((pairs, parts - 1)),
            ],
            compiler_params=pltpu.CompilerParams(
                collective_id=0, has_side_effects=True, vmem_limit_bytes=48 * 2**20
            ),
        )(layer_start, queries, train_grads)

    return jax.shard_map(
        body,
        mesh=mesh,
        in_specs=(P("ex", "layer"), P(("groups", "ex"), "layer"), P()),
        out_specs=P(("groups", "ex", "layer"), None),
        check_vma=False,
    )
```

```python
import functools

import jax
import jax.numpy as jnp
from jax import lax
from jax.experimental import pallas as pl
from jax.experimental.pallas import tpu as pltpu
from jax.sharding import PartitionSpec as P

WIDTH = 16384
EPSILON = 1e-05
MESH = pl.DeviceIdType.MESH
LANES = 128


def nt_dot(a, b):
    return lax.dot_general(a, b, (((1,), (1,)), ((), ())), preferred_element_type=jnp.float32)


def kernel(
    n, groups, parts, chunks, swapped, start_hbm, q_ref, x_hbm, out_ref,
    start_ref, x_v, scaled_v, q_all, sums, sums_in, inv_v, acc, acc_in,
    start_sem, x_sem, q_sem, z_send, z_recv, y_send, y_recv, sum_send, sum_recv, acc_send, acc_recv,
):
    y, z, me = lax.axis_index("groups"), lax.axis_index("ex"), lax.axis_index("layer")
    rows, width = q_ref.shape
    share = rows // groups
    chunk = width // chunks
    examples = x_hbm.shape[0]
    kept = examples // parts
    layers = start_hbm.shape[0]
    last = n - 2
    pairs = n // 2

    def cols(c):
        return pl.ds(c * chunk, chunk)

    def x_copy(c):
        return pltpu.make_async_copy(x_hbm.at[:, cols(c)], x_v.at[:, cols(c)], x_sem.at[c])

    def block_rows(b):
        return pl.ds(pl.multiple_of(b * rows, rows), rows)

    def q_copy(c):
        return pltpu.make_async_copy(q_ref.at[:, cols(c)], q_all.at[c, block_rows(z)], q_sem.at[c])

    def share_rows(b, g):
        return pl.ds(pl.multiple_of(b * rows + g * share, share), share)

    def z_target(flow):
        return z + 1 if flow == 0 else z - 1

    def has_target(flow):
        return z + 1 < n if flow == 0 else z > 0

    def arriving(flow, s):
        return z - 1 - s if flow == 0 else z + 1 + s

    def arrives(flow, s):
        return z - 1 - s >= 0 if flow == 0 else z + 1 + s < n

    def is_edge(flow, b):
        return b == (0 if flow == 0 else n - 1)

    def by_kind(flow, b, c, act):
        if c < swapped:
            act(False)
        else:
            edge = is_edge(flow, b)
            pl.when(edge)(lambda: act(True))
            pl.when(jnp.logical_not(edge))(lambda: act(False))

    def z_copy(flow, s, c, b, whole, own=False):
        there = q_all.at[c, block_rows(b) if whole else share_rows(b, y)]
        here = there
        if own:
            here = q_ref.at[:, cols(c)] if whole else q_ref.at[pl.ds(pl.multiple_of(y * share, share), share), cols(c)]
        return pltpu.make_async_remote_copy(
            src_ref=here, dst_ref=there, send_sem=z_send.at[flow, s], recv_sem=z_recv.at[flow, s, c],
            device_id={"ex": z_target(flow)}, device_id_type=MESH)

    def y_copy(flow, s, g, c, b, owner):
        block = q_all.at[c, share_rows(b, owner)]
        return pltpu.make_async_remote_copy(
            src_ref=block, dst_ref=block, send_sem=y_send.at[flow, s, g - 1], recv_sem=y_recv.at[flow, s, g - 1, c],
            device_id={"groups": lax.rem(y + g, groups)}, device_id_type=MESH)

    def sum_copy(r):
        return pltpu.make_async_remote_copy(
            src_ref=sums, dst_ref=sums_in.at[r - 1], send_sem=sum_send.at[r - 1], recv_sem=sum_recv.at[r - 1],
            device_id={"layer": lax.rem(me + r, parts)}, device_id_type=MESH)

    def acc_copy(k, r):
        to = lax.rem(me + r, parts)
        return pltpu.make_async_remote_copy(
            src_ref=acc.at[k, pl.ds(pl.multiple_of(to * kept, 8), kept)], dst_ref=acc_in.at[k, r - 1],
            send_sem=acc_send.at[k, r - 1], recv_sem=acc_recv.at[k, r - 1],
            device_id={"layer": to}, device_id_type=MESH)

    def z_sends(flow, s):
        return has_target(flow) if s == 0 else has_target(flow) & arrives(flow, s - 1)

    def wait_sends(s):
        def wait(due, semaphore, count):
            if count:
                @pl.when(due)
                def _():
                    lead = pl.cdiv(count, n * rows)
                    sent = q_all.at[pl.ds(0, lead), pl.ds(0, count // lead)]
                    pltpu.make_async_copy(sent, sent, semaphore).wait()

        full, less, more = chunks * share, swapped * share, swapped * share + (chunks - swapped) * rows
        for flow in (1, 0):
            edge = is_edge(flow, z if s == 0 else arriving(flow, s - 1))
            wait(z_sends(flow, s) & edge, z_send.at[flow, s], more)
            wait(z_sends(flow, s) & jnp.logical_not(edge), z_send.at[flow, s], full)
            edge = is_edge(flow, arriving(flow, s))
            for g in range(1, groups):
                wait(arrives(flow, s) & edge, y_send.at[flow, s, g - 1], less)
                wait(arrives(flow, s) & jnp.logical_not(edge), y_send.at[flow, s, g - 1], full)

    def handle(s, c):
        for flow in (1, 0):
            b = arriving(flow, s)

            def act(whole):
                z_copy(flow, s, c, b, whole).wait_recv()
                if not whole:
                    for g in range(1, groups):
                        y_copy(flow, s, g, c, b, y).start()
                if s < last:
                    @pl.when(has_target(flow))
                    def _():
                        z_copy(flow, s + 1, c, b, whole).start()

            @pl.when(arrives(flow, s))
            def _():
                by_kind(flow, b, c, act)

    def wait_y(s, c):
        for flow in (1, 0):
            b = arriving(flow, s)
            due = arrives(flow, s)
            if c >= swapped:
                due = due & jnp.logical_not(is_edge(flow, b))

            @pl.when(due)
            def _():
                for g in range(1, groups):
                    y_copy(flow, s, g, c, b, lax.rem(y + groups - g, groups)).wait_recv()

    start_copy = pltpu.make_async_copy(start_hbm, start_ref, start_sem)
    start_copy.start()
    for c in range(chunks):
        x_copy(c).start()
    for c in range(chunks):
        q_copy(c).start()

    barrier = pltpu.get_barrier_semaphore()
    for flow in (0, 1):
        @pl.when(has_target(flow))
        def _():
            pl.semaphore_signal(barrier, inc=1, device_id={"ex": z_target(flow)}, device_id_type=MESH)
    for g in range(1, groups):
        pl.semaphore_signal(barrier, inc=1, device_id={"groups": lax.rem(y + g, groups)}, device_id_type=MESH)
    for r in range(1, parts):
        pl.semaphore_signal(barrier, inc=1, device_id={"layer": lax.rem(me + r, parts)}, device_id_type=MESH)
    peers = groups + parts - jnp.where(z == 0, 1, 0) - jnp.where(z == n - 1, 1, 0)
    pl.semaphore_wait(barrier, peers)

    for c in range(chunks):
        for flow in (1, 0):
            @pl.when(has_target(flow))
            def _():
                by_kind(flow, z, c, lambda whole: z_copy(flow, 0, c, z, whole, own=True).start())

    start_copy.wait()
    starts = [start_ref[l] for l in range(layers)]
    ends = starts[1:] + [WIDTH]
    offset = me * width

    def table(index):
        low = jnp.full(index.shape, WIDTH, jnp.int32)
        high = jnp.full(index.shape, 0, jnp.int32)
        for l in range(layers):
            low = jnp.where(index == l, starts[l], low)
            high = jnp.where(index == l, ends[l], high)
        return low - offset, high - offset

    lane_low, lane_high = table(lax.broadcasted_iota(jnp.int32, (1, LANES), 1))
    sub = lax.broadcasted_iota(jnp.int32, (LANES, 1), 0)
    pieces = 3
    sub_low, sub_high = table(jnp.where(sub < pieces * layers, lax.rem(sub, layers), layers))

    total = jnp.zeros((examples, LANES), jnp.float32)
    for c in range(chunks):
        x_copy(c).wait()
        column = c * chunk + lax.broadcasted_iota(jnp.int32, (chunk, LANES), 0)
        member = ((column >= lane_low) & (column < lane_high)).astype(jnp.float32).astype(jnp.bfloat16)
        wide = x_v[:, cols(c)].astype(jnp.float32)
        square = wide * wide
        big = square.astype(jnp.bfloat16)
        small = (square - big.astype(jnp.float32)).astype(jnp.bfloat16)
        total += jnp.dot(big, member, preferred_element_type=jnp.float32)
        total += jnp.dot(small, member, preferred_element_type=jnp.float32)
        handle(0, c)
    sums[...] = total.T[:layers]
    for r in range(1, parts):
        sum_copy(r).start()

    for c in range(chunks):
        q_copy(c).wait()
    own_pair = z // 2

    def pair_dot(k, p, c):
        pair = pl.ds(pl.multiple_of(p * 2 * rows, 2 * rows), 2 * rows)
        value = nt_dot(scaled_v[:, cols(c)], q_all[c, pair])
        if c == 0:
            acc[k] = value
        else:
            acc[k] += value

    def send_pair(k):
        for r in range(1, parts):
            acc_copy(k, r).start()

    for c in range(chunks):
        if last >= 1:
            handle(1, c)
        if c == 0:
            for r in range(1, parts):
                sum_copy(r).wait_recv()
            tot = sums[...]
            for r in range(1, parts):
                tot += sums_in[r - 1]
            low, high = sub_low[:layers], sub_high[:layers]
            counts = (high - low).astype(jnp.float32)
            overall = jnp.sum(tot, axis=0, keepdims=True) / WIDTH
            inv = lax.rsqrt(tot / counts + overall + EPSILON) * WIDTH ** (-0.5)
            split = []
            rest = inv
            for _ in range(pieces):
                piece = rest.astype(jnp.bfloat16).astype(jnp.float32)
                split.append(piece)
                rest = rest - piece
            split.append(jnp.zeros((LANES - pieces * layers, examples), jnp.float32))
            inv_v[...] = jnp.concatenate(split, axis=0).T.astype(jnp.bfloat16)
        column = c * chunk + lax.broadcasted_iota(jnp.int32, (LANES, chunk), 1)
        member = ((column >= sub_low) & (column < sub_high)).astype(jnp.float32).astype(jnp.bfloat16)
        scale = jnp.dot(inv_v[...], member, preferred_element_type=jnp.float32)
        scaled_v[:, cols(c)] = (x_v[:, cols(c)].astype(jnp.float32) * scale).astype(jnp.bfloat16)
        wait_y(0, c)
        pair_dot(0, own_pair, c)
    send_pair(0)

    ahead = z < n // 2
    last_pair = jnp.where(ahead, pairs - 1, 0)
    pair_of = [own_pair]
    for s in range(2, last):
        for c in range(chunks):
            handle(s, c)
    for c in range(swapped):
        handle(last, c)
    for s in range(1, last):
        for c in range(chunks):
            wait_y(s, c)
    for k in range(1, pairs - 1):
        p = jnp.where(ahead, k - 1, k)
        p = p + jnp.where(p >= own_pair, 1, 0)
        pair_of.append(p)
        for c in range(chunks):
            pair_dot(k, p, c)
        send_pair(k)
    pair_of.append(last_pair)
    for c in range(chunks):
        if c < swapped:
            wait_y(last, c)
        else:
            handle(last, c)
        pair_dot(pairs - 1, last_pair, c)
    send_pair(pairs - 1)

    for s in range(last + 1):
        wait_sends(s)
    for r in range(1, parts):
        sum_copy(r).wait_send()
    mine = pl.ds(pl.multiple_of(me * kept, 8), kept)
    for k in range(pairs):
        value = acc[k, mine]
        for r in range(1, parts):
            acc_copy(k, r).wait_recv()
            value += acc_in[k, r - 1]
        out_ref[:, pl.ds(pl.multiple_of(pair_of[k] * 2 * rows, 2 * rows), 2 * rows)] = value
    for k in range(pairs):
        for r in range(1, parts):
            acc_copy(k, r).wait_send()


def solution(mesh):
    n, groups, parts = mesh.shape["ex"], mesh.shape["groups"], mesh.shape["layer"]
    chunks = max(1, 16 // n)
    swapped = chunks - chunks // 2

    def body(queries, train_grads, layer_start):
        rows, width = queries.shape
        examples = train_grads.shape[0]
        layers = layer_start.shape[0]
        kept = examples // parts
        pairs = n // 2
        dma = pltpu.SemaphoreType.DMA
        return pl.pallas_call(
            functools.partial(kernel, n, groups, parts, chunks, swapped),
            out_shape=jax.ShapeDtypeStruct((kept, n * rows), jnp.float32),
            in_specs=[
                pl.BlockSpec(memory_space=pltpu.HBM),
                pl.BlockSpec(memory_space=pltpu.HBM),
                pl.BlockSpec(memory_space=pltpu.HBM),
            ],
            out_specs=pl.BlockSpec(memory_space=pltpu.VMEM),
            scratch_shapes=[
                pltpu.SMEM((layers,), jnp.int32),
                pltpu.VMEM((examples, width), jnp.bfloat16),
                pltpu.VMEM((examples, width), jnp.bfloat16),
                pltpu.VMEM((chunks, n * rows, width // chunks), jnp.bfloat16),
                pltpu.VMEM((layers, examples), jnp.float32),
                pltpu.VMEM((parts - 1, layers, examples), jnp.float32),
                pltpu.VMEM((examples, LANES), jnp.bfloat16),
                pltpu.VMEM((pairs, examples, 2 * rows), jnp.float32),
                pltpu.VMEM((pairs, parts - 1, kept, 2 * rows), jnp.float32),
                dma,
                dma((chunks,)),
                dma((chunks,)),
                dma((2, n - 1)),
                dma((2, n - 1, chunks)),
                dma((2, n - 1, groups - 1)),
                dma((2, n - 1, groups - 1, chunks)),
                dma((parts - 1,)),
                dma((parts - 1,)),
                dma((pairs, parts - 1)),
                dma((pairs, parts - 1)),
            ],
            compiler_params=pltpu.CompilerParams(
                collective_id=0, has_side_effects=True, vmem_limit_bytes=60 * 2**20
            ),
        )(layer_start, queries, train_grads)

    return jax.shard_map(
        body,
        mesh=mesh,
        in_specs=(P("ex", "layer"), P(("groups", "ex"), "layer"), P()),
        out_specs=P(("groups", "ex", "layer"), None),
        check_vma=False,
    )
```

```python
import functools

import jax
import jax.numpy as jnp
from jax import lax
from jax.experimental import pallas as pl
from jax.experimental.pallas import tpu as pltpu
from jax.sharding import PartitionSpec as P

WIDTH = 16384
EPSILON = 1e-05
MESH = pl.DeviceIdType.MESH
LANES = 128


def nt_dot(a, b):
    return lax.dot_general(a, b, (((1,), (1,)), ((), ())), preferred_element_type=jnp.float32)


def kernel(
    n, groups, parts, chunks, swapped, start_hbm, q_ref, x_hbm, out_ref,
    start_ref, x_v, scaled_v, q_all, sums, sums_in, inv_v, acc, acc_in, half, half_out, half_in,
    start_sem, x_sem, q_sem, z_send, z_recv, y_send, y_recv, sum_send, sum_recv, acc_send, acc_recv, half_send, half_recv,
):
    y, z, me = lax.axis_index("groups"), lax.axis_index("ex"), lax.axis_index("layer")
    rows, width = q_ref.shape
    share = rows // groups
    chunk = width // chunks
    examples = x_hbm.shape[0]
    kept = examples // parts
    layers = start_hbm.shape[0]
    last = n - 2
    pairs = n // 2

    def cols(c):
        return pl.ds(c * chunk, chunk)

    def x_copy(c):
        return pltpu.make_async_copy(x_hbm.at[:, cols(c)], x_v.at[:, cols(c)], x_sem.at[c])

    def block_rows(b):
        return pl.ds(pl.multiple_of(b * rows, rows), rows)

    def q_copy(c):
        return pltpu.make_async_copy(q_ref.at[:, cols(c)], q_all.at[c, block_rows(z)], q_sem.at[c])

    def share_rows(b, g):
        return pl.ds(pl.multiple_of(b * rows + g * share, share), share)

    def z_target(flow):
        return z + 1 if flow == 0 else z - 1

    def has_target(flow):
        return z + 1 < n if flow == 0 else z > 0

    def arriving(flow, s):
        return z - 1 - s if flow == 0 else z + 1 + s

    def arrives(flow, s):
        return z - 1 - s >= 0 if flow == 0 else z + 1 + s < n

    def is_edge(flow, b):
        return b == (0 if flow == 0 else n - 1)

    def by_kind(flow, b, c, act):
        if c < swapped:
            act(False)
        else:
            edge = is_edge(flow, b)
            pl.when(edge)(lambda: act(True))
            pl.when(jnp.logical_not(edge))(lambda: act(False))

    def z_copy(flow, s, c, b, whole, own=False):
        there = q_all.at[c, block_rows(b) if whole else share_rows(b, y)]
        here = there
        if own:
            here = q_ref.at[:, cols(c)] if whole else q_ref.at[pl.ds(pl.multiple_of(y * share, share), share), cols(c)]
        return pltpu.make_async_remote_copy(
            src_ref=here, dst_ref=there, send_sem=z_send.at[flow, s], recv_sem=z_recv.at[flow, s, c],
            device_id={"ex": z_target(flow)}, device_id_type=MESH)

    def y_copy(flow, s, g, c, b, owner):
        block = q_all.at[c, share_rows(b, owner)]
        return pltpu.make_async_remote_copy(
            src_ref=block, dst_ref=block, send_sem=y_send.at[flow, s, g - 1], recv_sem=y_recv.at[flow, s, g - 1, c],
            device_id={"groups": lax.rem(y + g, groups)}, device_id_type=MESH)

    def sum_copy(r):
        return pltpu.make_async_remote_copy(
            src_ref=sums, dst_ref=sums_in.at[r - 1], send_sem=sum_send.at[r - 1], recv_sem=sum_recv.at[r - 1],
            device_id={"layer": lax.rem(me + r, parts)}, device_id_type=MESH)

    def acc_copy(k, r):
        to = lax.rem(me + r, parts)
        return pltpu.make_async_remote_copy(
            src_ref=acc.at[k, pl.ds(pl.multiple_of(to * kept, 8), kept)], dst_ref=acc_in.at[k, r - 1],
            send_sem=acc_send.at[k, r - 1], recv_sem=acc_recv.at[k, r - 1],
            device_id={"layer": to}, device_id_type=MESH)

    def z_sends(flow, s):
        return has_target(flow) if s == 0 else has_target(flow) & arrives(flow, s - 1)

    def wait_sends(s):
        def wait(due, semaphore, count):
            if count:
                @pl.when(due)
                def _():
                    lead = pl.cdiv(count, n * rows)
                    sent = q_all.at[pl.ds(0, lead), pl.ds(0, count // lead)]
                    pltpu.make_async_copy(sent, sent, semaphore).wait()

        full, less, more = chunks * share, swapped * share, swapped * share + (chunks - swapped) * rows
        for flow in (1, 0):
            edge = is_edge(flow, z if s == 0 else arriving(flow, s - 1))
            wait(z_sends(flow, s) & edge, z_send.at[flow, s], more)
            wait(z_sends(flow, s) & jnp.logical_not(edge), z_send.at[flow, s], full)
            edge = is_edge(flow, arriving(flow, s))
            for g in range(1, groups):
                wait(arrives(flow, s) & edge, y_send.at[flow, s, g - 1], less)
                wait(arrives(flow, s) & jnp.logical_not(edge), y_send.at[flow, s, g - 1], full)

    def half_copy(i, r):
        return pltpu.make_async_remote_copy(
            src_ref=half_out.at[i, r - 1], dst_ref=half_in.at[i, r - 1],
            send_sem=half_send.at[i, r - 1], recv_sem=half_recv.at[i, r - 1],
            device_id={"layer": lax.rem(me + r, parts)}, device_id_type=MESH)

    def packed(i, to):
        value = half[i, pl.ds(pl.multiple_of(to * kept, 8), kept)]
        return jnp.concatenate([value[:kept // 2], value[kept // 2:]], axis=1)

    def send_half(i):
        for r in range(1, parts):
            half_out[i, r - 1] = packed(i, lax.rem(me + r, parts))
            half_copy(i, r).start()

    def half_dot(i, b, c):
        value = nt_dot(scaled_v[:, cols(c)], q_all[c, block_rows(b)])
        if c == 0:
            half[i] = value
        else:
            half[i] += value

    def half_total(i):
        value = packed(i, me)
        for r in range(1, parts):
            half_copy(i, r).wait_recv()
            value += half_in[i, r - 1]
        return jnp.concatenate([value[:, :rows], value[:, rows:]], axis=0)

    def handle(s, c):
        for flow in (1, 0):
            b = arriving(flow, s)

            def act(whole):
                z_copy(flow, s, c, b, whole).wait_recv()
                if not whole:
                    for g in range(1, groups):
                        y_copy(flow, s, g, c, b, y).start()
                if s < last:
                    @pl.when(has_target(flow))
                    def _():
                        z_copy(flow, s + 1, c, b, whole).start()

            @pl.when(arrives(flow, s))
            def _():
                by_kind(flow, b, c, act)

    def wait_y(s, c):
        for flow in (1, 0):
            b = arriving(flow, s)
            due = arrives(flow, s)
            if c >= swapped:
                due = due & jnp.logical_not(is_edge(flow, b))

            @pl.when(due)
            def _():
                for g in range(1, groups):
                    y_copy(flow, s, g, c, b, lax.rem(y + groups - g, groups)).wait_recv()

    start_copy = pltpu.make_async_copy(start_hbm, start_ref, start_sem)
    start_copy.start()
    for c in range(chunks):
        x_copy(c).start()
    for c in range(chunks):
        q_copy(c).start()

    barrier = pltpu.get_barrier_semaphore()
    for flow in (0, 1):
        @pl.when(has_target(flow))
        def _():
            pl.semaphore_signal(barrier, inc=1, device_id={"ex": z_target(flow)}, device_id_type=MESH)
    for g in range(1, groups):
        pl.semaphore_signal(barrier, inc=1, device_id={"groups": lax.rem(y + g, groups)}, device_id_type=MESH)
    for r in range(1, parts):
        pl.semaphore_signal(barrier, inc=1, device_id={"layer": lax.rem(me + r, parts)}, device_id_type=MESH)
    peers = groups + parts - jnp.where(z == 0, 1, 0) - jnp.where(z == n - 1, 1, 0)
    pl.semaphore_wait(barrier, peers)

    def send_own(c):
        for flow in (1, 0):
            @pl.when(has_target(flow))
            def _():
                by_kind(flow, z, c, lambda whole: z_copy(flow, 0, c, z, whole, own=True).start())

    ahead_sends = 2
    for c in range(min(ahead_sends, chunks)):
        send_own(c)

    start_copy.wait()
    starts = [start_ref[l] for l in range(layers)]
    ends = starts[1:] + [WIDTH]
    offset = me * width

    def table(index):
        low = jnp.full(index.shape, WIDTH, jnp.int32)
        high = jnp.full(index.shape, 0, jnp.int32)
        for l in range(layers):
            low = jnp.where(index == l, starts[l], low)
            high = jnp.where(index == l, ends[l], high)
        return low - offset, high - offset

    lane_low, lane_high = table(lax.broadcasted_iota(jnp.int32, (1, LANES), 1))
    sub = lax.broadcasted_iota(jnp.int32, (LANES, 1), 0)
    pieces = 3
    sub_low, sub_high = table(jnp.where(sub < pieces * layers, lax.rem(sub, layers), layers))

    total = jnp.zeros((examples, LANES), jnp.float32)
    for c in range(chunks):
        x_copy(c).wait()
        column = c * chunk + lax.broadcasted_iota(jnp.int32, (chunk, LANES), 0)
        member = ((column >= lane_low) & (column < lane_high)).astype(jnp.float32).astype(jnp.bfloat16)
        wide = x_v[:, cols(c)].astype(jnp.float32)
        square = wide * wide
        big = square.astype(jnp.bfloat16)
        small = (square - big.astype(jnp.float32)).astype(jnp.bfloat16)
        total += jnp.dot(big, member, preferred_element_type=jnp.float32)
        total += jnp.dot(small, member, preferred_element_type=jnp.float32)
        if c + ahead_sends < chunks:
            send_own(c + ahead_sends)
        if c:
            handle(0, c - 1)
    handle(0, chunks - 1)
    sums[...] = total.T[:layers]
    for r in range(1, parts):
        sum_copy(r).start()

    for c in range(chunks):
        q_copy(c).wait()
    own_pair = z // 2

    def pair_dot(k, p, c):
        pair = pl.ds(pl.multiple_of(p * 2 * rows, 2 * rows), 2 * rows)
        value = nt_dot(scaled_v[:, cols(c)], q_all[c, pair])
        if c == 0:
            acc[k] = value
        else:
            acc[k] += value

    def send_pair(k):
        for r in range(1, parts):
            acc_copy(k, r).start()

    for c in range(chunks):
        if last >= 1:
            handle(1, c)
        if c == 0:
            for r in range(1, parts):
                sum_copy(r).wait_recv()
            tot = sums[...]
            for r in range(1, parts):
                tot += sums_in[r - 1]
            low, high = sub_low[:layers], sub_high[:layers]
            counts = (high - low).astype(jnp.float32)
            overall = jnp.sum(tot, axis=0, keepdims=True) / WIDTH
            inv = lax.rsqrt(tot / counts + overall + EPSILON) * WIDTH ** (-0.5)
            split = []
            rest = inv
            for _ in range(pieces):
                piece = rest.astype(jnp.bfloat16).astype(jnp.float32)
                split.append(piece)
                rest = rest - piece
            split.append(jnp.zeros((LANES - pieces * layers, examples), jnp.float32))
            inv_v[...] = jnp.concatenate(split, axis=0).T.astype(jnp.bfloat16)
        column = c * chunk + lax.broadcasted_iota(jnp.int32, (LANES, chunk), 1)
        member = ((column >= sub_low) & (column < sub_high)).astype(jnp.float32).astype(jnp.bfloat16)
        scale = jnp.dot(inv_v[...], member, preferred_element_type=jnp.float32)
        scaled_v[:, cols(c)] = (x_v[:, cols(c)].astype(jnp.float32) * scale).astype(jnp.bfloat16)
        wait_y(0, c)
        pair_dot(0, own_pair, c)
    send_pair(0)

    ahead = z < n // 2
    last_pair = jnp.where(ahead, pairs - 1, 0)
    pair_of = [own_pair]
    for s in range(2, last):
        for c in range(chunks):
            handle(s, c)
    for c in range(swapped):
        handle(last, c)
    for s in range(1, last):
        for c in range(chunks):
            wait_y(s, c)
    for k in range(1, pairs - 1):
        p = jnp.where(ahead, k - 1, k)
        p = p + jnp.where(p >= own_pair, 1, 0)
        pair_of.append(p)
        for c in range(chunks):
            pair_dot(k, p, c)
        send_pair(k)
    near, far = jnp.where(ahead, n - 2, 1), jnp.where(ahead, n - 1, 0)
    for c in range(chunks):
        half_dot(0, near, c)
    send_half(0)
    for c in range(chunks):
        if c < swapped:
            wait_y(last, c)
        else:
            handle(last, c)
        half_dot(1, far, c)
    send_half(1)

    for s in range(last + 1):
        wait_sends(s)
    for r in range(1, parts):
        sum_copy(r).wait_send()
    mine = pl.ds(pl.multiple_of(me * kept, 8), kept)
    for k in range(pairs - 1):
        value = acc[k, mine]
        for r in range(1, parts):
            acc_copy(k, r).wait_recv()
            value += acc_in[k, r - 1]
        out_ref[:, pl.ds(pl.multiple_of(pair_of[k] * 2 * rows, 2 * rows), 2 * rows)] = value
    for r in range(1, parts):
        for k in range(pairs - 1):
            acc_copy(k, r).wait_send()
        half_copy(0, r).wait_send()
    near_total = half_total(0)
    far_total = half_total(1)
    first, second = jnp.where(ahead, near_total, far_total), jnp.where(ahead, far_total, near_total)
    out_ref[:, pl.ds(pl.multiple_of(last_pair * 2 * rows, 2 * rows), 2 * rows)] = jnp.concatenate([first, second], axis=1)
    for r in range(1, parts):
        half_copy(1, r).wait_send()


def solution(mesh):
    n, groups, parts = mesh.shape["ex"], mesh.shape["groups"], mesh.shape["layer"]
    chunks = max(1, 16 // n)
    swapped = chunks - chunks // 2

    def body(queries, train_grads, layer_start):
        rows, width = queries.shape
        examples = train_grads.shape[0]
        layers = layer_start.shape[0]
        kept = examples // parts
        pairs = n // 2
        dma = pltpu.SemaphoreType.DMA
        return pl.pallas_call(
            functools.partial(kernel, n, groups, parts, chunks, swapped),
            out_shape=jax.ShapeDtypeStruct((kept, n * rows), jnp.float32),
            in_specs=[
                pl.BlockSpec(memory_space=pltpu.HBM),
                pl.BlockSpec(memory_space=pltpu.HBM),
                pl.BlockSpec(memory_space=pltpu.HBM),
            ],
            out_specs=pl.BlockSpec(memory_space=pltpu.VMEM),
            scratch_shapes=[
                pltpu.SMEM((layers,), jnp.int32),
                pltpu.VMEM((examples, width), jnp.bfloat16),
                pltpu.VMEM((examples, width), jnp.bfloat16),
                pltpu.VMEM((chunks, n * rows, width // chunks), jnp.bfloat16),
                pltpu.VMEM((layers, examples), jnp.float32),
                pltpu.VMEM((parts - 1, layers, examples), jnp.float32),
                pltpu.VMEM((examples, LANES), jnp.bfloat16),
                pltpu.VMEM((pairs - 1, examples, 2 * rows), jnp.float32),
                pltpu.VMEM((pairs - 1, parts - 1, kept, 2 * rows), jnp.float32),
                pltpu.VMEM((2, examples, rows), jnp.float32),
                pltpu.VMEM((2, parts - 1, kept // 2, 2 * rows), jnp.float32),
                pltpu.VMEM((2, parts - 1, kept // 2, 2 * rows), jnp.float32),
                dma,
                dma((chunks,)),
                dma((chunks,)),
                dma((2, n - 1)),
                dma((2, n - 1, chunks)),
                dma((2, n - 1, groups - 1)),
                dma((2, n - 1, groups - 1, chunks)),
                dma((parts - 1,)),
                dma((parts - 1,)),
                dma((pairs - 1, parts - 1)),
                dma((pairs - 1, parts - 1)),
                dma((2, parts - 1)),
                dma((2, parts - 1)),
            ],
            compiler_params=pltpu.CompilerParams(
                collective_id=0, has_side_effects=True, vmem_limit_bytes=60 * 2**20
            ),
        )(layer_start, queries, train_grads)

    return jax.shard_map(
        body,
        mesh=mesh,
        in_specs=(P("ex", "layer"), P(("groups", "ex"), "layer"), P()),
        out_specs=P(("groups", "ex", "layer"), None),
        check_vma=False,
    )
```
